256 devices in a mesh: tm: 2 (over z_lo), lat: 16 (over z_hi, y), lon: 8 (over x, core).
Axes of the slice: x: 4, y: 4, z: 8 (z_hi: 4, z_lo: 2; z = z_hi * 2 + z_lo), core: 2. Of those that a mesh axis runs over, the one named last changes fastest.
Arguments:
- control: bfloat16 [1024, 2, 4, 8, 2048], P('lat', 'tm', None, None, 'lon'), may hold values from -6 to 6
- deviations: float32 [1024, 2, 4, 8, 2048], P('lat', 'tm', None, None, 'lon'), may hold values from 0.3 to 3
- increments: float32 [1024, 2, 4, 8, 2048], P('lat', 'tm', None, None, 'lon'), may hold values from -6 to 6
- lon_corr: bfloat16 [2048, 2048], P('lon'), may hold values from -0.125 to 0.125
- lat_corr: bfloat16 [1024, 1024], P('lat'), may hold values from -0.1875 to 0.1875
- offsets: int32 [2, 8], replicated, may hold values from -2 to 2, as said below
- courant: float32 [4], replicated, may hold values from 0.2 to 0.8
Outputs:
- misfit: float32 [1024, 2, 4, 8, 2048], P('lat', 'tm', None, None, 'lon')
The draws below stay inside these ranges and needn't reach their ends.
Inputs may be any that keep to these rules, and one draw needn't show every extreme that they name: `offsets`: each of the two rows holds both -2 and 2.
All inputs are finite; a program needn't handle non-finite values.
Results may differ from the reference program's by a relative error of at most 0.0024.
Values may be sent and summed in bfloat16 or wider, within the bound.
No kernel may reach another device: no remote copies, remote signals or barrier semaphores. Data moves between devices by JAX's collectives and lax.ppermute only.
A program may use at most 128 MiB of HBM per device.

```python
import math
import jax
import jax.numpy as jnp
from jax import lax

NLAT = 1024
NLON = 2048
LEV = 8
NVAR = 4
TSLOTS = 2


def draw_offsets(key, part):
    subkeys = jax.random.split(jax.random.fold_in(key, 7), 2)
    values_drawn = jax.random.randint(subkeys[0], (2, LEV), -2, 3)
    offset_rows = []
    for which_dim in range(2):
        ordering = jax.random.permutation(jax.random.fold_in(subkeys[1], which_dim), LEV)
        offset_row = values_drawn[which_dim].at[ordering[0]].set(-2).at[ordering[1]].set(2)
        offset_rows.append(offset_row)
    return jnp.stack(offset_rows, axis=0).astype(jnp.int32)


def steps_of(own_key, dims, pieces, low, largest):
    factor_of = 1.0
    for axis_at, blocks in pieces:
        heights = jax.random.uniform(jax.random.fold_in(jax.random.fold_in(own_key, 6), axis_at), (blocks,), jnp.float32, low / len(pieces), largest / len(pieces))
        factor_of = factor_of * jnp.repeat(jnp.exp(heights), dims[axis_at] // blocks).reshape((-1,) + (1,) * (len(dims) - 1 - axis_at))
    return factor_of


def bell_draw(rng, dims, width, limit, cuts=(), dtype=jnp.bfloat16):
    entries = jax.random.normal(rng, dims, jnp.float32) * width
    if len(cuts) > 0:
        entries = steps_of(rng, dims, cuts, -0.22, 0.18) * entries
    return jnp.clip(entries, min=-limit, max=limit).astype(dtype)


def setup_inputs(seed: int = 0) -> dict:
    arg_keys = jax.random.split(jax.random.key(seed), 8)
    control = bell_draw(arg_keys[0], (NLAT, TSLOTS, NVAR, LEV, NLON), 1.0, 6.0, ((0, 16), (1, 2), (4, 8)))
    deviations = jnp.clip(jnp.exp(math.log(3.0) - 2.3025851 * jax.random.uniform(arg_keys[1], (NLAT, TSLOTS, NVAR, LEV, NLON), jnp.float32) ** steps_of(arg_keys[1], (NLAT, TSLOTS, NVAR, LEV, NLON), ((0, 16), (1, 2), (4, 8)), -0.2, 0.2)), 0.3, 3.0)
    increments = bell_draw(arg_keys[2], (NLAT, TSLOTS, NVAR, LEV, NLON), 1.0, 6.0, ((0, 16), (1, 2), (4, 8)), jnp.float32)
    lon_corr = bell_draw(arg_keys[3], (NLON, NLON), NLON ** -0.5, 0.125, ((0, 8),))
    lat_corr = bell_draw(arg_keys[4], (NLAT, NLAT), NLAT ** -0.5, 0.1875, ((0, 16),))
    offsets = draw_offsets(jax.random.fold_in(arg_keys[7], 71), 0)
    courant = jnp.clip(jax.random.uniform(arg_keys[6], (NVAR,), jnp.float32, 0.2, 0.8), 0.2, 0.8)
    return dict(control=control, deviations=deviations, increments=increments, lon_corr=lon_corr, lat_corr=lat_corr, offsets=offsets, courant=courant)


def advect(field_now, offsets, courant):
    padded = jnp.pad(field_now, ((2, 2), (0, 0), (0, 0), (0, 0), (0, 0)))
    padded = jnp.concatenate([padded[..., -2:], padded, padded[..., :2]], axis=4)
    displaced_all = []
    for level_idx in range(LEV):
        one_level = padded[:, :, :, level_idx, :]
        displaced = lax.dynamic_slice_in_dim(one_level, (2 - offsets[0, level_idx]).astype(jnp.int32), NLAT, 0)
        displaced = lax.dynamic_slice_in_dim(displaced, (2 - offsets[1, level_idx]).astype(jnp.int32), NLON, 3)
        displaced_all.append(displaced)
    shifted = jnp.stack(displaced_all, axis=3)
    blending = courant.reshape(1, 1, -1, 1, 1)
    return (1.0 - blending) * field_now + blending * shifted


def reference(control, deviations, increments, lon_corr, lat_corr, offsets, courant):
    flat_rows = control.reshape(-1, NLON)
    smoothed = lax.dot_general(flat_rows, lon_corr, (((1,), (1,)), ((), ())), preferred_element_type=jnp.float32)
    halfway = smoothed.astype(jnp.bfloat16).reshape(NLAT, -1)
    correlated = jnp.dot(lat_corr, halfway, preferred_element_type=jnp.float32)
    forcing = deviations * correlated.reshape(control.shape)
    evolved = advect(increments, offsets, courant)
    previous = jnp.concatenate([jnp.zeros_like(evolved[:, :1]), evolved[:, :-1]], axis=1)
    return increments - previous - forcing
```

```python
import functools

import jax
import jax.numpy as jnp
from jax import lax
from jax.experimental import pallas as pl
from jax.experimental.pallas import tpu as pltpu
from jax.sharding import Mesh, PartitionSpec as P

F32, BF16 = jnp.float32, jnp.bfloat16
VMEM_LIMIT = 48 * 1024 * 1024
NT = (((1,), (1,)), ((), ()))


def call(kernel, out_shape, n_in, smem=(), scratch=(), before=(), work=0):
    def run(*refs):
        kernel(*refs[:n_in], *refs[n_in + len(before) :])

    in_specs = [
        pl.BlockSpec(memory_space=pltpu.SMEM if k in smem else pltpu.VMEM) for k in range(n_in)
    ] + [pl.BlockSpec(memory_space=pl.ANY)] * len(before)
    made = pl.pallas_call(
        run,
        out_shape=out_shape,
        in_specs=in_specs,
        out_specs=jax.tree.map(lambda _: pl.BlockSpec(memory_space=pltpu.VMEM), out_shape),
        scratch_shapes=list(scratch),
        compiler_params=pltpu.CompilerParams(vmem_limit_bytes=VMEM_LIMIT),
        cost_estimate=pl.CostEstimate(flops=0, bytes_accessed=work, transcendentals=0),
    )
    return lambda *args: made(*args, *before)


def after(value, *before):
    anywhere = pl.BlockSpec(memory_space=pl.ANY)
    return pl.pallas_call(
        lambda *refs: None,
        out_shape=jax.ShapeDtypeStruct(value.shape, value.dtype),
        in_specs=[anywhere] * (1 + len(before)),
        out_specs=anywhere,
        input_output_aliases={0: 0},
    )(value, *before)


def split_kernel(control, out, wide):
    for side in range(2):
        at = slice(side * 128, (side + 1) * 128)
        wide[side] = control[:, 0, :, at].astype(F32).reshape(512, 128)
    for level in range(8):
        for side in range(2):
            at = slice(side * 128, (side + 1) * 128)
            rows = wide[side, pl.ds(level, 64, stride=8), :].astype(BF16)
            out[level * 4 : (level + 1) * 4, :, at] = rows.reshape(4, 16, 128)


def smooth_kernel(place, mine, other, own, behind, ahead, across, keep, send):
    core, side = place[4], place[5]
    for k in range(4):
        corr = (own, behind, ahead, across)[k]
        for rows, at in ((mine, core), (other, 1 - core)):
            total = None
            for q in range(8):
                term = lax.dot_general(
                    rows[:, q].reshape(256, 256),
                    corr[:, q * 256 : (q + 1) * 256],
                    NT,
                    preferred_element_type=F32,
                )
                total = term if total is None else total + term
            total = total.astype(BF16)
            low, high = total[:, :128], total[:, 128:]
            keep[place[k], at] = jnp.where(side == 0, low, high)
            send[place[k], at] = jnp.where(side == 0, high, low)


def correlate_kernel(place, lat, kept, got, out):
    side = place[5]
    for block in range(4):
        at = slice(block * 256, (block + 1) * 256)
        for pair in range(2):
            total = None
            for cols, where in ((kept, side), (got, 1 - side)):
                for part in range(2):
                    left = lat[at, pl.ds(pl.multiple_of((where * 2 + part) * 256, 256), 256)]
                    right = jnp.concatenate([cols[pair * 2, part], cols[pair * 2 + 1, part]], axis=1)
                    term = jnp.dot(left, right, preferred_element_type=F32)
                    total = term if total is None else total + term
            total = total.astype(BF16)
            for k in range(4):
                for j in range(2):
                    out[(block * 4 + k) * 4 + pair * 2 + j] = total[
                        k * 64 : (k + 1) * 64, j * 128 : (j + 1) * 128
                    ]


def advect_kernel(inc, field, low, high, left, right, off0, off1, courant, out, padded):
    lane = lax.broadcasted_iota(jnp.int32, (4, 8, 128), 2)

    def fill(a, _):
        padded[a + 2, :, :, :256] = field[a].astype(F32)
        return 0

    lax.fori_loop(0, 64, fill, 0)
    padded[0:2, :, :, :256] = low[...].astype(F32)
    padded[66:68, :, :, :256] = high[...].astype(F32)

    def rim(a, _):
        padded[a, :, :, 256:] = jnp.where(lane < 64, right[a].astype(F32), left[a].astype(F32))
        return 0

    lax.fori_loop(0, 68, rim, 0)
    row_off = jnp.broadcast_to(off0[...][None], (4, 8, 384))
    col_off = jnp.broadcast_to(off1[...][None], (4, 8, 384))
    blend = courant[...]

    def step(a, _):
        at = padded[a + 2]
        moved = at
        for d in (-2, -1, 1, 2):
            moved = jnp.where(row_off == d, padded[a + 2 - d], moved)
        shifted = moved
        for d in (-2, -1, 1, 2):
            rolled = pltpu.roll(moved.reshape(32, 384), d % 384, 1).reshape(4, 8, 384)
            shifted = jnp.where(col_off == d, rolled, shifted)
        evolved = (1.0 - blend) * at[:, :, :256] + blend * shifted[:, :, :256]
        out[a] = inc[a] - evolved
        return 0

    lax.fori_loop(0, 64, step, 0)


def final_kernel(base, dev, got, out, acc):
    rows = base.shape[0]
    for v in range(4):
        for half in range(2):
            at = slice(half * 128, (half + 1) * 128)
            for level in range(8):
                row = got[(v * 8 + level) * 2 + half].astype(F32)
                acc[half, pl.ds(level, rows, stride=8), :] = row
            corr = acc[half].reshape(rows, 8, 128)
            out[:, v, :, at] = base[:, v, :, at] - dev[:, v, :, at] * corr


def body(control, deviations, increments, lon_corr, lat_corr, offsets, courant):
    x, c = lax.axis_index("x"), lax.axis_index("c")
    swap = [(0, 1), (1, 0)]
    lats = ("zh", "y")

    def along_x(v, s):
        return lax.ppermute(v, "x", [(i, (i + s) % 4) for i in range(4)])

    behind, ahead, across = (along_x(lon_corr, s) for s in (1, -1, 2))
    place = jnp.stack([x, (x + 3) % 4, (x + 1) % 4, (x + 2) % 4, c, x % 2]).astype(jnp.int32)

    parts = pl.pallas_call(
        split_kernel,
        grid=(4,),
        out_shape=jax.ShapeDtypeStruct((128, 16, 256), BF16),
        in_specs=[pl.BlockSpec((64, 1, 8, 256), lambda v: (0, v, 0, 0))],
        out_specs=pl.BlockSpec((32, 16, 256), lambda v: (v, 0, 0)),
        scratch_shapes=[pltpu.VMEM((2, 512, 128), F32)],
        compiler_params=pltpu.CompilerParams(vmem_limit_bytes=VMEM_LIMIT),
        cost_estimate=pl.CostEstimate(flops=0, bytes_accessed=0, transcendentals=0),
    )(control.reshape(64, 4, 8, 256))
    mine = lax.all_to_all(parts, ("zh", "y", "x", "c"), 0, 0, tiled=True)
    mine = mine.reshape(16, 8, 16, 256)
    other = lax.ppermute(mine, "c", swap)

    lat = lat_corr.reshape(64, 16, 4, 16).transpose(0, 2, 1, 3).reshape(64, 1024)
    lat = lax.all_gather(lat, lats, axis=0, tiled=True)

    inc = increments.reshape(64, 4, 8, 256)
    dev = deviations.reshape(64, 4, 8, 256)
    field = lax.ppermute(after(inc.astype(BF16), mine), "tm", [(0, 1)])
    low = lax.ppermute(field[62:], lats, [(i, i + 1) for i in range(15)])
    high = lax.ppermute(field[:2], lats, [(i + 1, i) for i in range(15)])
    wide = jnp.concatenate([low, field, high], axis=0)
    ring = [(i, (i + 1) % 8) for i in range(8)]
    back = [((i + 1) % 8, i) for i in range(8)]
    left = lax.ppermute(wide[..., 128:], ("x", "c"), ring)
    right = lax.ppermute(wide[..., :128], ("x", "c"), back)
    off = jnp.broadcast_to(offsets[:, :, None], (2, 8, 384))
    base = call(
        advect_kernel,
        jax.ShapeDtypeStruct((64, 4, 8, 256), F32),
        9,
        scratch=[pltpu.VMEM((68, 4, 8, 384), F32)],
        work=30_000_000,
    )(
        inc, field, low, high, left, right, off[0], off[1],
        jnp.broadcast_to(courant[:, None, None], (4, 8, 256)),
    )

    half = jax.ShapeDtypeStruct((4, 2, 256, 128), BF16)
    keep, send = call(smooth_kernel, (half, half), 7, smem=(0,))(
        place, mine, other, lon_corr, behind, ahead, across
    )
    got = lax.ppermute(send, "x", [(i, i ^ 1) for i in range(4)])
    res = call(
        correlate_kernel, jax.ShapeDtypeStruct((64, 64, 128), BF16), 4, smem=(0,), before=(field,)
    )(place, lat, keep, got)
    res = lax.all_to_all(res, ("zh", "y", "x"), 0, 0, tiled=True)

    big = pl.BlockSpec((16, 4, 8, 256), lambda i: (i, 0, 0, 0))
    out = pl.pallas_call(
        final_kernel,
        grid=(4,),
        out_shape=jax.ShapeDtypeStruct((64, 4, 8, 256), F32),
        in_specs=[big, big, pl.BlockSpec((64, 16, 128), lambda i: (0, i, 0))],
        out_specs=big,
        scratch_shapes=[pltpu.VMEM((2, 128, 128), F32)],
        compiler_params=pltpu.CompilerParams(vmem_limit_bytes=VMEM_LIMIT),
        cost_estimate=pl.CostEstimate(flops=0, bytes_accessed=0, transcendentals=0),
    )(base, dev, res)
    return out.reshape(increments.shape)


def solution(mesh):
    fine = Mesh(mesh.devices.reshape(2, 4, 4, 4, 2), ("tm", "zh", "y", "x", "c"))
    lat, lon = ("zh", "y"), ("x", "c")
    tile = P(lat, "tm", None, None, lon)
    in_specs = (tile, tile, tile, P(lon, None), P(lat, None), P(), P())
    return jax.shard_map(body, mesh=fine, in_specs=in_specs, out_specs=tile, check_vma=False)
```

```python
import functools

import jax
import jax.numpy as jnp
from jax import lax
from jax.experimental import pallas as pl
from jax.experimental.pallas import tpu as pltpu
from jax.sharding import Mesh, PartitionSpec as P

F32, BF16 = jnp.float32, jnp.bfloat16
VMEM_LIMIT = 48 * 1024 * 1024
NT = (((1,), (1,)), ((), ()))


def call(kernel, out_shape, n_in, smem=(), scratch=(), before=(), work=0):
    def run(*refs):
        kernel(*refs[:n_in], *refs[n_in + len(before) :])

    in_specs = [
        pl.BlockSpec(memory_space=pltpu.SMEM if k in smem else pltpu.VMEM) for k in range(n_in)
    ] + [pl.BlockSpec(memory_space=pl.ANY)] * len(before)
    made = pl.pallas_call(
        run,
        out_shape=out_shape,
        in_specs=in_specs,
        out_specs=jax.tree.map(lambda _: pl.BlockSpec(memory_space=pltpu.VMEM), out_shape),
        scratch_shapes=list(scratch),
        compiler_params=pltpu.CompilerParams(vmem_limit_bytes=VMEM_LIMIT),
        cost_estimate=pl.CostEstimate(flops=0, bytes_accessed=work, transcendentals=0),
    )
    return lambda *args: made(*args, *before)


def after(value, *before):
    anywhere = pl.BlockSpec(memory_space=pl.ANY)
    return pl.pallas_call(
        lambda *refs: None,
        out_shape=jax.ShapeDtypeStruct(value.shape, value.dtype),
        in_specs=[anywhere] * (1 + len(before)),
        out_specs=anywhere,
        input_output_aliases={0: 0},
    )(value, *before)


def split_kernel(control, out, wide):
    for side in range(2):
        at = slice(side * 128, (side + 1) * 128)
        wide[side] = control[:, 0, :, at].astype(F32).reshape(512, 128)
    for level in range(8):
        for side in range(2):
            at = slice(side * 128, (side + 1) * 128)
            rows = wide[side, pl.ds(level, 64, stride=8), :].astype(BF16)
            out[level * 4 : (level + 1) * 4, :, at] = rows.reshape(4, 16, 128)


def smooth(rows, near, far):
    made = []
    for corr in (near, far):
        total = None
        for q in range(8):
            term = lax.dot_general(
                rows[:, q].reshape(256, 256),
                corr[:, q * 256 : (q + 1) * 256],
                NT,
                preferred_element_type=F32,
            )
            total = term if total is None else total + term
        made.append(total.astype(BF16))
    return made


def smooth_kernel(rows0, rows1, near, far, out):
    for k, rows in enumerate((rows0, rows1)):
        for tile, value in enumerate(smooth(rows, near, far)):
            out[k, tile] = value


def correlate_kernel(place, lat0, lat1, done, rows2, rows3, near, far, out, cols):
    for k in range(4):
        made = smooth((rows2, rows3)[k - 2], near, far) if k > 1 else (done[k, 0], done[k, 1])
        at = pl.ds(pl.multiple_of(place[1 + k] * 256, 256), 256)
        for tile, value in enumerate(made):
            cols[tile, at] = value
    for block in range(4):
        for tile in range(2):
            total = None
            for k, lat in enumerate((lat0, lat1)):
                at = pl.ds(pl.multiple_of(place[5 + k] * 512, 512), 512)
                left = lat[block * 256 : (block + 1) * 256]
                term = jnp.dot(left, cols[tile, at], preferred_element_type=F32)
                total = term if total is None else total + term
            total = total.astype(BF16)
            where = jnp.where(place[0] == 0, tile, 1 - tile)
            for k in range(4):
                out[(block * 4 + k) * 2 + where] = total[k * 64 : (k + 1) * 64]


def advect_kernel(inc, field, rim, off0, off1, courant, out, padded):
    step = pl.program_id(0)
    rows = inc.shape[0]

    @pl.when(step == 0)
    def _():
        def fill(a, _):
            padded[a, :, :, :256] = field[a].astype(F32)
            padded[a, :, :, 256:] = rim[a].astype(F32)
            return 0

        lax.fori_loop(0, 68, fill, 0, unroll=4)

    row_off = jnp.broadcast_to(off0[...][None], (4, 8, 384))
    col_off = jnp.broadcast_to(off1[...][None], (4, 8, 384))
    blend = courant[...]

    def one(k, _):
        a = step * rows + k
        at = padded[a + 2]
        moved = at
        for d in (-2, -1, 1, 2):
            moved = jnp.where(row_off == d, padded[a + 2 - d], moved)
        shifted = moved
        for d in (-2, -1, 1, 2):
            rolled = pltpu.roll(moved.reshape(32, 384), d % 384, 1).reshape(4, 8, 384)
            shifted = jnp.where(col_off == d, rolled, shifted)
        evolved = (1.0 - blend) * inc[k] + blend * shifted[:, :, :256]
        out[k] = evolved.astype(BF16)
        return 0

    lax.fori_loop(0, rows, one, 0, unroll=2)


def final_kernel(inc, past, dev, got, out, acc):
    rows = inc.shape[0]
    for v in range(4):
        for half in range(2):
            at = slice(half * 128, (half + 1) * 128)
            for level in range(8):
                row = got[v * 8 + level, :, at].astype(F32)
                acc[half, pl.ds(level, rows, stride=8), :] = row
            corr = acc[half].reshape(rows, 8, 128)
            rest = inc[:, v, :, at] - past[:, v, :, at].astype(F32)
            out[:, v, :, at] = rest - dev[:, v, :, at] * corr


def body(control, deviations, increments, lon_corr, lat_corr, offsets, courant):
    xh, xl, c = (lax.axis_index(name) for name in ("xh", "xl", "c"))
    swap = [(0, 1), (1, 0)]
    lats = ("zh", "y")
    params = pltpu.CompilerParams(vmem_limit_bytes=VMEM_LIMIT)
    free = pl.CostEstimate(flops=0, bytes_accessed=0, transcendentals=0)

    inc = increments.reshape(64, 4, 8, 256)

    across = lax.ppermute(lon_corr, "xh", swap)

    parts = pl.pallas_call(
        split_kernel,
        grid=(4,),
        out_shape=jax.ShapeDtypeStruct((128, 16, 256), BF16),
        in_specs=[pl.BlockSpec((64, 1, 8, 256), lambda v: (0, v, 0, 0))],
        out_specs=pl.BlockSpec((32, 16, 256), lambda v: (v, 0, 0)),
        scratch_shapes=[pltpu.VMEM((2, 512, 128), F32)],
        compiler_params=params,
        cost_estimate=free,
    )(control.reshape(64, 4, 8, 256))
    low = lax.ppermute(inc[62:].astype(BF16), lats, [(i, i + 1) for i in range(15)])
    high = lax.ppermute(inc[:2].astype(BF16), lats, [(i + 1, i) for i in range(15)])
    mine = lax.all_to_all(parts, ("zh", "y", "xh", "xl", "c"), 0, 0, tiled=True)
    wide = jnp.concatenate([low, inc.astype(BF16), high], axis=0)
    ring = [(i, (i + 1) % 8) for i in range(8)]
    back = [((i + 1) % 8, i) for i in range(8)]
    left = lax.ppermute(wide[..., 254:], ("xh", "xl", "c"), ring)
    right = lax.ppermute(wide[..., :2], ("xh", "xl", "c"), back)
    rim = jnp.concatenate([right, jnp.zeros((68, 4, 8, 124), BF16), left], axis=-1)
    off = jnp.broadcast_to(offsets[:, :, None], (2, 8, 384))
    big = pl.BlockSpec((16, 4, 8, 256), lambda i: (i, 0, 0, 0))
    evolved = pl.pallas_call(
        advect_kernel,
        grid=(4,),
        out_shape=jax.ShapeDtypeStruct((64, 4, 8, 256), BF16),
        in_specs=[big] + [pl.BlockSpec(memory_space=pltpu.VMEM)] * 5,
        out_specs=big,
        scratch_shapes=[pltpu.VMEM((68, 4, 8, 384), F32)],
        compiler_params=params,
        cost_estimate=pl.CostEstimate(flops=0, bytes_accessed=20_000_000, transcendentals=0),
    )(inc, wide, rim, off[0], off[1], jnp.broadcast_to(courant[:, None, None], (4, 8, 256)))

    mine = after(mine.reshape(16, 8, 16, 256), across, evolved)
    past = lax.ppermute(after(evolved, mine), "tm", [(0, 1)])
    paired = lax.ppermute(mine, "xl", swap)
    sibling = lax.ppermute(mine, "c", swap)
    opposite = lax.ppermute(paired, "c", swap)
    quarters = [xl * 2 + c, xl * 2 + 1 - c, 2 - 2 * xl + c, 3 - 2 * xl - c]
    place = jnp.stack([xh] + quarters + [c, 1 - c]).astype(jnp.int32)

    lat = lat_corr.reshape(64, 16, 4, 16).transpose(0, 2, 1, 3).reshape(64, 2, 512)
    lat = lax.dynamic_index_in_dim(lat, c, 1, keepdims=False)
    lat0 = lax.all_gather(lat, lats, axis=0, tiled=True)
    lat0 = after(lat0, paired)
    lat1 = lax.ppermute(lat0, "c", swap)

    dev = deviations.reshape(64, 4, 8, 256)
    made = jax.ShapeDtypeStruct((2, 2, 256, 256), BF16)
    done = call(smooth_kernel, made, 4, work=30_000_000)(mine, sibling, lon_corr, across)
    res = call(
        correlate_kernel,
        jax.ShapeDtypeStruct((32, 64, 256), BF16),
        8,
        smem=(0,),
        scratch=[pltpu.VMEM((2, 1024, 256), BF16)],
        before=(past,),
    )(place, lat0, lat1, done, paired, opposite, lon_corr, across)
    res = lax.all_to_all(res, ("zh", "y", "xh"), 0, 0, tiled=True)

    out = pl.pallas_call(
        final_kernel,
        grid=(4,),
        out_shape=jax.ShapeDtypeStruct((64, 4, 8, 256), F32),
        in_specs=[big, big, big, pl.BlockSpec((32, 16, 256), lambda i: (0, i, 0))],
        out_specs=big,
        scratch_shapes=[pltpu.VMEM((2, 128, 128), F32)],
        compiler_params=params,
        cost_estimate=free,
    )(inc, past, dev, res)
    return out.reshape(increments.shape)


def solution(mesh):
    fine = Mesh(mesh.devices.reshape(2, 4, 4, 2, 2, 2), ("tm", "zh", "y", "xh", "xl", "c"))
    lat, lon = ("zh", "y"), ("xh", "xl", "c")
    tile = P(lat, "tm", None, None, lon)
    in_specs = (tile, tile, tile, P(lon, None), P(lat, None), P(), P())
    return jax.shard_map(body, mesh=fine, in_specs=in_specs, out_specs=tile, check_vma=False)
```

```python
import functools

import jax
import jax.numpy as jnp
from jax import lax
from jax.experimental import pallas as pl
from jax.experimental.pallas import tpu as pltpu
from jax.sharding import Mesh, PartitionSpec as P

F32, BF16 = jnp.float32, jnp.bfloat16
VMEM_LIMIT = 48 * 1024 * 1024
NT = (((1,), (1,)), ((), ()))


def call(kernel, out_shape, n_in, smem=(), scratch=(), before=(), work=0):
    def run(*refs):
        kernel(*refs[:n_in], *refs[n_in + len(before) :])

    in_specs = [
        pl.BlockSpec(memory_space=pltpu.SMEM if k in smem else pltpu.VMEM) for k in range(n_in)
    ] + [pl.BlockSpec(memory_space=pl.ANY)] * len(before)
    made = pl.pallas_call(
        run,
        out_shape=out_shape,
        in_specs=in_specs,
        out_specs=jax.tree.map(lambda _: pl.BlockSpec(memory_space=pltpu.VMEM), out_shape),
        scratch_shapes=list(scratch),
        compiler_params=pltpu.CompilerParams(vmem_limit_bytes=VMEM_LIMIT),
        cost_estimate=pl.CostEstimate(flops=0, bytes_accessed=work, transcendentals=0),
    )
    return lambda *args: made(*args, *before)


def after(value, *before):
    anywhere = pl.BlockSpec(memory_space=pl.ANY)
    return pl.pallas_call(
        lambda *refs: None,
        out_shape=jax.ShapeDtypeStruct(value.shape, value.dtype),
        in_specs=[anywhere] * (1 + len(before)),
        out_specs=anywhere,
        input_output_aliases={0: 0},
    )(value, *before)


def split_kernel(control, out, wide):
    for side in range(2):
        at = slice(side * 128, (side + 1) * 128)
        wide[side] = control[:, 0, :, at].astype(F32).reshape(512, 128)
    for level in range(8):
        for side in range(2):
            at = slice(side * 128, (side + 1) * 128)
            out[level, :, at] = wide[side, pl.ds(level, 64, stride=8), :].astype(BF16)


def smooth(starts, pieces, corr, block):
    total = None
    for start, piece in zip(starts, pieces):
        for k in range(2):
            term = lax.dot_general(
                piece[block * 4 : (block + 1) * 4, k].reshape(256, 256),
                corr[:, pl.ds(pl.multiple_of(start + k * 512, 256), 256)],
                NT,
                preferred_element_type=F32,
            )
            total = term if total is None else total + term
    return total


def smooth_kernel(place, rows0, rows1, near, far, out):
    for tile, corr in enumerate((near, far)):
        for block in range(4):
            at = slice(block * 256, (block + 1) * 256)
            out[tile, at] = smooth((place[1], place[2]), (rows0, rows1), corr, block)


def correlate_kernel(place, lat0, lat1, begun, rows2, rows3, near, far, out, cols):
    for tile, corr in enumerate((near, far)):
        for block in range(4):
            at = slice(block * 256, (block + 1) * 256)
            rest = smooth((place[3], place[4]), (rows2, rows3), corr, block)
            cols[tile, at] = (begun[tile, at] + rest).astype(BF16)
    for block in range(4):
        for tile in range(2):
            total = None
            for k, lat in enumerate((lat0, lat1)):
                at = pl.ds(pl.multiple_of(place[5 + k] * 512, 512), 512)
                left = lat[block * 256 : (block + 1) * 256]
                term = jnp.dot(left, cols[tile, at], preferred_element_type=F32)
                total = term if total is None else total + term
            total = total.astype(BF16)
            where = jnp.where(place[0] == 0, tile, 1 - tile)
            for k in range(4):
                out[(block * 4 + k) * 2 + where] = total[k * 64 : (k + 1) * 64]


def advect_kernel(inc, field, rim, off0, off1, courant, out, padded):
    step = pl.program_id(0)
    rows = inc.shape[0]

    @pl.when(step == 0)
    def _():
        def fill(a, _):
            padded[a, :, :, :256] = field[a].astype(F32)
            padded[a, :, :, 256:] = rim[a].astype(F32)
            return 0

        lax.fori_loop(0, 68, fill, 0, unroll=4)

    row_off = jnp.broadcast_to(off0[...][None], (4, 8, 384))
    col_off = jnp.broadcast_to(off1[...][None], (4, 8, 384))
    blend = courant[...]

    def one(k, _):
        a = step * rows + k
        at = padded[a + 2]
        moved = at
        for d in (-2, -1, 1, 2):
            moved = jnp.where(row_off == d, padded[a + 2 - d], moved)
        shifted = moved
        for d in (-2, -1, 1, 2):
            rolled = pltpu.roll(moved.reshape(32, 384), d % 384, 1).reshape(4, 8, 384)
            shifted = jnp.where(col_off == d, rolled, shifted)
        evolved = (1.0 - blend) * at[:, :, :256] + blend * shifted[:, :, :256]
        out[k] = inc[k] - evolved
        return 0

    lax.fori_loop(0, rows, one, 0, unroll=2)


def final_kernel(turned, base, dev, got, out, acc):
    rows = base.shape[0]
    for v in range(4):
        for half in range(2):
            at = slice(half * 128, (half + 1) * 128)
            for level in range(8):
                row = got[v * 8 + jnp.bitwise_xor(level, turned[0]), :, at].astype(F32)
                acc[half, pl.ds(level, rows, stride=8), :] = row
            corr = acc[half].reshape(rows, 8, 128)
            out[:, v, :, at] = base[:, v, :, at] - dev[:, v, :, at] * corr


def body(control, deviations, increments, lon_corr, lat_corr, offsets, courant):
    xh, xl, c = (lax.axis_index(name) for name in ("xh", "xl", "c"))
    swap = [(0, 1), (1, 0)]
    lats = ("zh", "y")
    params = pltpu.CompilerParams(vmem_limit_bytes=VMEM_LIMIT)
    free = pl.CostEstimate(flops=0, bytes_accessed=0, transcendentals=0)

    inc = increments.reshape(64, 4, 8, 256)

    across = lax.ppermute(lon_corr, ("xh", "xl"), [(i, 3 - i) for i in range(4)])

    lat = lax.dynamic_slice_in_dim(lat_corr, c * 512, 512, 1)
    parts = pl.pallas_call(
        lambda control, lat, out, wide: split_kernel(control, out, wide),
        grid=(4,),
        out_shape=jax.ShapeDtypeStruct((32, 64, 256), BF16),
        in_specs=[
            pl.BlockSpec((64, 1, 8, 256), lambda v: (0, v, 0, 0)),
            pl.BlockSpec(memory_space=pl.ANY),
        ],
        out_specs=pl.BlockSpec((8, 64, 256), lambda v: (v, 0, 0)),
        scratch_shapes=[pltpu.VMEM((2, 512, 128), F32)],
        compiler_params=params,
        cost_estimate=free,
    )(control.reshape(64, 4, 8, 256), lat)
    low = lax.ppermute(inc[62:].astype(BF16), lats, [(i, i + 1) for i in range(15)])
    high = lax.ppermute(inc[:2].astype(BF16), lats, [(i + 1, i) for i in range(15)])
    mine = lax.all_to_all(parts, ("zh", "y", "xl"), 0, 0, tiled=True)
    mine = after(mine.reshape(16, 2, 64, 256), across, low, high)
    paired = lax.ppermute(mine, "xh", swap)
    sibling = lax.ppermute(mine, "c", swap)
    opposite = lax.ppermute(paired, "c", swap)
    starts = [(a * 4 + b) * 256 for a in (xh, 1 - xh) for b in (c, 1 - c)]
    place = jnp.stack([xh] + starts + [c, 1 - c]).astype(jnp.int32)

    lat0 = after(lax.all_gather(lat, lats, axis=0, tiled=True), paired)
    lat1 = lax.ppermute(lat0, "c", swap)

    dev = deviations.reshape(64, 4, 8, 256)
    wide = jnp.concatenate([low, inc.astype(BF16), high], axis=0)
    wide = lax.ppermute(wide, "tm", [(0, 1)])
    ring = [(i, (i + 1) % 8) for i in range(8)]
    back = [((i + 1) % 8, i) for i in range(8)]
    left = lax.ppermute(wide[..., 254:], ("xh", "xl", "c"), ring)
    right = lax.ppermute(wide[..., :2], ("xh", "xl", "c"), back)
    rim = jnp.concatenate([right, jnp.zeros((68, 4, 8, 124), BF16), left], axis=-1)
    off = jnp.broadcast_to(offsets[:, :, None], (2, 8, 384))
    big = pl.BlockSpec((16, 4, 8, 256), lambda i: (i, 0, 0, 0))
    base = pl.pallas_call(
        advect_kernel,
        grid=(4,),
        out_shape=jax.ShapeDtypeStruct((64, 4, 8, 256), F32),
        in_specs=[big] + [pl.BlockSpec(memory_space=pltpu.VMEM)] * 5,
        out_specs=big,
        scratch_shapes=[pltpu.VMEM((68, 4, 8, 384), F32)],
        compiler_params=params,
        cost_estimate=pl.CostEstimate(flops=0, bytes_accessed=20_000_000, transcendentals=0),
    )(inc, wide, rim, off[0], off[1], jnp.broadcast_to(courant[:, None, None], (4, 8, 256)))

    made = jax.ShapeDtypeStruct((2, 1024, 256), F32)
    begun = call(smooth_kernel, made, 5, smem=(0,), work=30_000_000)(
        place, mine, sibling, lon_corr, across
    )
    res = call(
        correlate_kernel,
        jax.ShapeDtypeStruct((32, 64, 256), BF16),
        8,
        smem=(0,),
        scratch=[pltpu.VMEM((2, 1024, 256), BF16)],
        before=(wide,),
    )(place, lat0, lat1, begun, paired, opposite, lon_corr, across)
    groups = [[p * 4 + k for p in range(16) for k in pair] for pair in ((0, 3), (1, 2))]
    res = lax.all_to_all(
        res, ("zh", "y", "xh", "xl"), 0, 0, axis_index_groups=groups, tiled=True
    )
    turned = jnp.stack([jnp.bitwise_xor(xh, xl)]).astype(jnp.int32)

    out = pl.pallas_call(
        final_kernel,
        grid=(4,),
        out_shape=jax.ShapeDtypeStruct((64, 4, 8, 256), F32),
        in_specs=[pl.BlockSpec(memory_space=pltpu.SMEM), big, big, pl.BlockSpec((32, 16, 256), lambda i: (0, i, 0))],
        out_specs=big,
        scratch_shapes=[pltpu.VMEM((2, 128, 128), F32)],
        compiler_params=params,
        cost_estimate=free,
    )(turned, base, dev, res)
    return out.reshape(increments.shape)


def solution(mesh):
    fine = Mesh(mesh.devices.reshape(2, 4, 4, 2, 2, 2), ("tm", "zh", "y", "xh", "xl", "c"))
    lat, lon = ("zh", "y"), ("xh", "xl", "c")
    tile = P(lat, "tm", None, None, lon)
    in_specs = (tile, tile, tile, P(lon, None), P(lat, None), P(), P())
    return jax.shard_map(body, mesh=fine, in_specs=in_specs, out_specs=tile, check_vma=False)
```

```python
import functools

import jax
import jax.numpy as jnp
from jax import lax
from jax.experimental import pallas as pl
from jax.experimental.pallas import tpu as pltpu
from jax.sharding import Mesh, PartitionSpec as P

F32, BF16 = jnp.float32, jnp.bfloat16
VMEM_LIMIT = 48 * 1024 * 1024
NT = (((1,), (1,)), ((), ()))


def call(kernel, out_shape, n_in, smem=(), scratch=(), before=(), work=0):
    def run(*refs):
        kernel(*refs[:n_in], *refs[n_in + len(before) :])

    in_specs = [
        pl.BlockSpec(memory_space=pltpu.SMEM if k in smem else pltpu.VMEM) for k in range(n_in)
    ] + [pl.BlockSpec(memory_space=pl.ANY)] * len(before)
    made = pl.pallas_call(
        run,
        out_shape=out_shape,
        in_specs=in_specs,
        out_specs=jax.tree.map(lambda _: pl.BlockSpec(memory_space=pltpu.VMEM), out_shape),
        scratch_shapes=list(scratch),
        compiler_params=pltpu.CompilerParams(vmem_limit_bytes=VMEM_LIMIT),
        cost_estimate=pl.CostEstimate(flops=0, bytes_accessed=work, transcendentals=0),
    )
    return lambda *args: made(*args, *before)


def after(value, *before):
    anywhere = pl.BlockSpec(memory_space=pl.ANY)
    return pl.pallas_call(
        lambda *refs: None,
        out_shape=jax.ShapeDtypeStruct(value.shape, value.dtype),
        in_specs=[anywhere] * (1 + len(before)),
        out_specs=anywhere,
        input_output_aliases={0: 0},
    )(value, *before)


def split_kernel(control, out, wide):
    for side in range(2):
        at = slice(side * 128, (side + 1) * 128)
        wide[side] = control[:, 0, :, at].astype(F32).reshape(512, 128)
    for level in range(8):
        for side in range(2):
            at = slice(side * 128, (side + 1) * 128)
            out[level, :, at] = wide[side, pl.ds(level, 64, stride=8), :].astype(BF16)


def smooth(starts, pieces, corr, block):
    total = None
    for start, piece in zip(starts, pieces):
        for k in range(2):
            term = lax.dot_general(
                piece[block * 4 : (block + 1) * 4, k].reshape(256, 256),
                corr[:, pl.ds(pl.multiple_of(start + k * 512, 256), 256)],
                NT,
                preferred_element_type=F32,
            )
            total = term if total is None else total + term
    return total


def smooth_kernel(place, rows0, rows1, near, far, out):
    for tile, corr in enumerate((near, far)):
        for block in range(4):
            at = slice(block * 256, (block + 1) * 256)
            out[tile, at] = smooth((place[1], place[2]), (rows0, rows1), corr, block)


def correlate_kernel(place, lat0, lat1, begun, rows2, rows3, near, far, out, cols):
    for tile, corr in enumerate((near, far)):
        for block in range(4):
            at = slice(block * 256, (block + 1) * 256)
            rest = smooth((place[3], place[4]), (rows2, rows3), corr, block)
            cols[tile, at] = (begun[tile, at] + rest).astype(BF16)
    for block in range(4):
        for tile in range(2):
            total = None
            for k, lat in enumerate((lat0, lat1)):
                at = pl.ds(pl.multiple_of(place[5 + k] * 512, 512), 512)
                left = lat[block * 256 : (block + 1) * 256]
                term = jnp.dot(left, cols[tile, at], preferred_element_type=F32)
                total = term if total is None else total + term
            total = total.astype(BF16)
            where = jnp.where(place[0] == 0, tile, 1 - tile)
            for k in range(4):
                out[(block * 4 + k) * 2 + where] = total[k * 64 : (k + 1) * 64]


def advect_kernel(inc, field, rim, off0, off1, courant, out, padded):
    step = pl.program_id(0)
    rows = inc.shape[0]

    @pl.when(step == 0)
    def _():
        def fill(a, _):
            padded[a, :, :, :256] = field[a].astype(F32)
            padded[a, :, :, 256:] = rim[a].astype(F32)
            return 0

        lax.fori_loop(0, 68, fill, 0, unroll=4)

    row_off = jnp.broadcast_to(off0[...][None], (4, 8, 384))
    col_off = jnp.broadcast_to(off1[...][None], (4, 8, 384))
    blend = courant[...]

    def one(k, _):
        a = step * rows + k
        at = padded[a + 2]
        moved = at
        for d in (-2, -1, 1, 2):
            moved = jnp.where(row_off == d, padded[a + 2 - d], moved)
        shifted = moved
        for d in (-2, -1, 1, 2):
            rolled = pltpu.roll(moved.reshape(32, 384), d % 384, 1).reshape(4, 8, 384)
            shifted = jnp.where(col_off == d, rolled, shifted)
        evolved = (1.0 - blend) * at[:, :, :256] + blend * shifted[:, :, :256]
        out[k] = inc[k] - evolved
        return 0

    lax.fori_loop(0, rows, one, 0, unroll=2)


def final_kernel(turned, base, dev, got, out, acc):
    rows = base.shape[0]
    for v in range(4):
        for half in range(2):
            at = slice(half * 128, (half + 1) * 128)
            for level in range(8):
                row = got[v * 8 + jnp.bitwise_xor(level, turned[0]), :, at].astype(F32)
                acc[half, pl.ds(level, rows, stride=8), :] = row
            corr = acc[half].reshape(rows, 8, 128)
            out[:, v, :, at] = base[:, v, :, at] - dev[:, v, :, at] * corr


def body(control, deviations, increments, lon_corr, lat_corr, offsets, courant):
    xh, xl, c = (lax.axis_index(name) for name in ("xh", "xl", "c"))
    swap = [(0, 1), (1, 0)]
    lats = ("zh", "y")
    params = pltpu.CompilerParams(vmem_limit_bytes=VMEM_LIMIT)
    free = pl.CostEstimate(flops=0, bytes_accessed=0, transcendentals=0)

    inc = increments.reshape(64, 4, 8, 256)

    across = lax.ppermute(lon_corr, ("xh", "xl"), [(i, 3 - i) for i in range(4)])

    lat = lax.dynamic_slice_in_dim(lat_corr, c * 512, 512, 1)
    parts = pl.pallas_call(
        lambda control, lat, out, wide: split_kernel(control, out, wide),
        grid=(4,),
        out_shape=jax.ShapeDtypeStruct((32, 64, 256), BF16),
        in_specs=[
            pl.BlockSpec((64, 1, 8, 256), lambda v: (0, v, 0, 0)),
            pl.BlockSpec(memory_space=pl.ANY),
        ],
        out_specs=pl.BlockSpec((8, 64, 256), lambda v: (v, 0, 0)),
        scratch_shapes=[pltpu.VMEM((2, 512, 128), F32)],
        compiler_params=params,
        cost_estimate=free,
    )(control.reshape(64, 4, 8, 256), lat)
    low = lax.ppermute(inc[62:].astype(BF16), lats, [(i, i + 1) for i in range(15)])
    high = lax.ppermute(inc[:2].astype(BF16), lats, [(i + 1, i) for i in range(15)])
    mine = lax.all_to_all(parts, ("zh", "y", "xl"), 0, 0, tiled=True)
    wide = jnp.concatenate([low, inc.astype(BF16), high], axis=0)
    mine = after(mine.reshape(16, 2, 64, 256), across, wide)
    paired = lax.ppermute(mine, "xh", swap)
    sibling = lax.ppermute(mine, "c", swap)
    starts = [(a * 4 + b) * 256 for a in (xh, 1 - xh) for b in (c, 1 - c)]
    place = jnp.stack([xh] + starts + [c, 1 - c]).astype(jnp.int32)

    made = jax.ShapeDtypeStruct((2, 1024, 256), F32)
    begun = call(smooth_kernel, made, 5, smem=(0,), work=30_000_000)(
        place, mine, sibling, lon_corr, across
    )
    paired = after(paired, begun)
    opposite = lax.ppermute(paired, "c", swap)

    lat0 = after(lax.all_gather(lat, lats, axis=0, tiled=True), paired)
    lat1 = lax.ppermute(lat0, "c", swap)

    dev = deviations.reshape(64, 4, 8, 256)
    wide = lax.ppermute(wide, "tm", [(0, 1)])
    ring = [(i, (i + 1) % 8) for i in range(8)]
    back = [((i + 1) % 8, i) for i in range(8)]
    left = lax.ppermute(wide[..., 254:], ("xh", "xl", "c"), ring)
    right = lax.ppermute(wide[..., :2], ("xh", "xl", "c"), back)
    rim = jnp.concatenate([right, jnp.zeros((68, 4, 8, 124), BF16), left], axis=-1)
    off = jnp.broadcast_to(offsets[:, :, None], (2, 8, 384))
    big = pl.BlockSpec((16, 4, 8, 256), lambda i: (i, 0, 0, 0))
    base = pl.pallas_call(
        advect_kernel,
        grid=(4,),
        out_shape=jax.ShapeDtypeStruct((64, 4, 8, 256), F32),
        in_specs=[big] + [pl.BlockSpec(memory_space=pltpu.VMEM)] * 5,
        out_specs=big,
        scratch_shapes=[pltpu.VMEM((68, 4, 8, 384), F32)],
        compiler_params=params,
        cost_estimate=pl.CostEstimate(flops=0, bytes_accessed=20_000_000, transcendentals=0),
    )(inc, wide, rim, off[0], off[1], jnp.broadcast_to(courant[:, None, None], (4, 8, 256)))

    res = call(
        correlate_kernel,
        jax.ShapeDtypeStruct((32, 64, 256), BF16),
        8,
        smem=(0,),
        scratch=[pltpu.VMEM((2, 1024, 256), BF16)],
        before=(wide,),
    )(place, lat0, lat1, begun, paired, opposite, lon_corr, across)
    groups = [[p * 4 + k for p in range(16) for k in pair] for pair in ((0, 3), (1, 2))]
    res = lax.all_to_all(
        res, ("zh", "y", "xh", "xl"), 0, 0, axis_index_groups=groups, tiled=True
    )
    turned = jnp.stack([jnp.bitwise_xor(xh, xl)]).astype(jnp.int32)

    out = pl.pallas_call(
        final_kernel,
        grid=(4,),
        out_shape=jax.ShapeDtypeStruct((64, 4, 8, 256), F32),
        in_specs=[pl.BlockSpec(memory_space=pltpu.SMEM), big, big, pl.BlockSpec((32, 16, 256), lambda i: (0, i, 0))],
        out_specs=big,
        scratch_shapes=[pltpu.VMEM((2, 128, 128), F32)],
        compiler_params=pltpu.CompilerParams(vmem_limit_bytes=62 * 1024 * 1024),
        cost_estimate=free,
    )(turned, base, dev, res)
    return out.reshape(increments.shape)


def solution(mesh):
    fine = Mesh(mesh.devices.reshape(2, 4, 4, 2, 2, 2), ("tm", "zh", "y", "xh", "xl", "c"))
    lat, lon = ("zh", "y"), ("xh", "xl", "c")
    tile = P(lat, "tm", None, None, lon)
    in_specs = (tile, tile, tile, P(lon, None), P(lat, None), P(), P())
    return jax.shard_map(body, mesh=fine, in_specs=in_specs, out_specs=tile, check_vma=False)
```
